128 devices in a mesh: fsdp: 8 (over z, core), tp: 16 (over y, x).
Axes of the slice: x: 4, y: 4, z: 4, core: 2. Of those that a mesh axis runs over, the one named last changes fastest.
Arguments:
- base_projection: bfloat16 [2, 16384, 18432], P(None, ('fsdp', 'tp')), may hold values from -6 to 6
- down_factor_transposed: bfloat16 [2, 64, 16384], P(None, None, ('fsdp', 'tp')), may hold values from -2 to 2
- up_factor: bfloat16 [2, 64, 18432], P(None, 'fsdp'), may hold values from -6 to 6
- block_permutation: int32 [144], replicated, may hold values from 0 to 143, each once
Outputs:
- merged: bfloat16 [2, 16384, 18432], P(None, 'fsdp', 'tp')
The draws below stay inside these ranges and needn't reach their ends.
Inputs may be any that keep to these rules, and one draw needn't show every extreme that they name: `block_permutation`: each block index appears exactly once.
All inputs are finite; a program needn't handle non-finite values.
Results may differ from the reference program's by a relative error of at most 0.001.
Values may be sent and summed in bfloat16 or wider, within the bound.
No kernel may reach another device: no remote copies, remote signals or barrier semaphores. Data moves between devices by JAX's collectives and lax.ppermute only.
A program may use at most 128 MiB of HBM per device.

```python
import jax
import jax.numpy as jnp

MODEL_WIDTH = 16384
UPDATE_RANK = 64
WINDOW_LAYERS = 2
BLOCK = 128
QUERY_KEY_VALUE = 18432
QBLK = 144


def levels(key, shape, cuts, smallest, largest):
    loudness, own = 1.0, jax.random.fold_in(key, 6)
    for axis_at, shards_of in cuts:
        heights = jnp.exp(jax.random.uniform(jax.random.fold_in(own, axis_at), (shards_of,), jnp.float32, smallest / len(cuts), largest / len(cuts)))
        loudness = loudness * jnp.repeat(heights, shape[axis_at] // shards_of).reshape([-1 if axis == axis_at else 1 for axis in range(len(shape))])
    return loudness


def bell_draw(rng, extent, width, bound, pieces=(), held_as=jnp.bfloat16):
    result = jax.random.normal(rng, extent, jnp.float32) * width
    if len(pieces) > 0:
        result = levels(rng, extent, pieces, -0.22, 0.18) * result
    return jnp.clip(result, min=-bound, max=bound).astype(held_as)


def setup_inputs(seed: int = 0) -> dict:
    streams_of = jax.random.split(jax.random.key(seed), 5)
    return {
        "base_projection": bell_draw(streams_of[0], (WINDOW_LAYERS, MODEL_WIDTH, QUERY_KEY_VALUE), 1.0, 6.0, ((1, 128),)),
        "down_factor_transposed": bell_draw(streams_of[1], (WINDOW_LAYERS, UPDATE_RANK, MODEL_WIDTH), 0.125, 2.0, ((2, 128),)),
        "up_factor": bell_draw(streams_of[2], (WINDOW_LAYERS, UPDATE_RANK, QUERY_KEY_VALUE), 0.5, 6.0, ((1, 8),)),
        "block_permutation": jax.random.permutation(streams_of[3], QBLK).astype(jnp.int32),
    }


update_scale = 2.0


def permute_columns(values, order):
    lead = values.shape[:-1]
    blocks = values.reshape(lead + (QBLK, BLOCK))
    blocks = jnp.take(blocks, order, axis=-2)
    return blocks.reshape(lead + (QUERY_KEY_VALUE,))


def reference(base_projection, down_factor_transposed, up_factor, block_permutation):
    merged_outputs = []
    for layer_index in range(WINDOW_LAYERS):
        permuted_base = permute_columns(base_projection[layer_index], block_permutation)
        permuted_up_factor = permute_columns(up_factor[layer_index], block_permutation)
        update_product = jnp.dot(down_factor_transposed[layer_index].T, permuted_up_factor, preferred_element_type=jnp.float32)
        merged_outputs.append((permuted_base.astype(jnp.float32) + update_scale * update_product).astype(jnp.bfloat16))
    return jnp.stack(merged_outputs)
```

```python
import jax
import jax.numpy as jnp
from jax import lax
from jax.experimental import pallas as pl
from jax.experimental.pallas import tpu as pltpu
from jax.sharding import PartitionSpec as P

BLOCK = 128
STRIPE = 32
VMEM_BYTES = 60 << 20


def block_at(order, j):
    return pl.ds(pl.multiple_of(order[j] * BLOCK, BLOCK), BLOCK)


def pack(order, base, down, servers):
    layers, rows, columns = base.shape
    per_server = order.shape[0] // servers
    chunk = layers * per_server + 1
    stripes = rows // STRIPE

    def kernel(order, base, down, out, held, packed, load_sem, store_sem):
        def load(s):
            return pltpu.make_async_copy(
                base.at[s // stripes, pl.ds(s % stripes * STRIPE, STRIPE)], held.at[s], load_sem.at[s]
            )

        def store(blocks, at):
            return pltpu.make_async_copy(packed.at[:, blocks, at], out.at[:, blocks, at], store_sem.at[0])

        for s in range(layers * stripes):
            load(s).start()
        for d in range(servers):
            packed[d, chunk - 1] = down[...]
        store(pl.ds(chunk - 1, 1), pl.ds(0, rows)).start()
        for s in range(layers * stripes):
            layer, at = s // stripes, pl.ds(s % stripes * STRIPE, STRIPE)
            load(s).wait()

            @pl.loop(0, servers)
            def _(d):
                for c in range(per_server):
                    packed[d, layer * per_server + c, at] = held[s, :, block_at(order, d * per_server + c)]

            store(pl.ds(layer * per_server, per_server), at).start()
        pltpu.make_async_copy(packed, out, store_sem.at[0]).wait()

    return pl.pallas_call(
        kernel,
        out_shape=jax.ShapeDtypeStruct((servers, chunk, rows, BLOCK), jnp.bfloat16),
        in_specs=[
            pl.BlockSpec(memory_space=pltpu.SMEM),
            pl.BlockSpec(memory_space=pltpu.HBM),
            pl.BlockSpec(memory_space=pltpu.VMEM),
        ],
        out_specs=pl.BlockSpec(memory_space=pltpu.HBM),
        scratch_shapes=[
            pltpu.VMEM((layers * stripes, STRIPE, columns), jnp.bfloat16),
            pltpu.VMEM((servers, chunk, rows, BLOCK), jnp.bfloat16),
            pltpu.SemaphoreType.DMA((layers * stripes,)),
            pltpu.SemaphoreType.DMA((1,)),
        ],
        compiler_params=pltpu.CompilerParams(vmem_limit_bytes=VMEM_BYTES),
        name="pack",
    )(order, base, down)


def merge(order, received, up):
    servers, chunk, rows, _ = received.shape
    layers, ranks, _ = up.shape
    per_server = (chunk - 1) // layers
    width = per_server * BLOCK

    def kernel(order, received, up, out, chosen, held, merged, up_sem, load_sem, store_sem):
        first = lax.axis_index("tp") * per_server
        for c in range(per_server):
            pltpu.make_async_copy(
                up.at[:, :, block_at(order, first + c)],
                chosen.at[:, :, pl.ds(c * BLOCK, BLOCK)],
                up_sem.at[0],
            ).start()

        def load(s):
            return pltpu.make_async_copy(received.at[s], held.at[s], load_sem.at[s])

        for s in range(servers):
            load(s).start()
        pltpu.make_async_copy(chosen, chosen, up_sem.at[0]).wait()

        @pl.loop(0, servers)
        def _(s):
            load(s).wait()
            at = pl.ds(pl.multiple_of(s * rows, rows), rows)
            for layer in range(layers):
                delta = lax.dot_general(
                    held[s, chunk - 1, layer * ranks : (layer + 1) * ranks] * jnp.bfloat16(2),
                    chosen[layer],
                    (((0,), (0,)), ((), ())),
                    preferred_element_type=jnp.float32,
                )
                for c in range(per_server):
                    columns = slice(c * BLOCK, (c + 1) * BLOCK)
                    base = held[s, layer * per_server + c].astype(jnp.float32)
                    merged[layer, at, columns] = (base + delta[:, columns]).astype(jnp.bfloat16)
            pltpu.make_async_copy(merged.at[:, at], out.at[:, at], store_sem.at[0]).start()

        pltpu.make_async_copy(merged, out, store_sem.at[0]).wait()

    return pl.pallas_call(
        kernel,
        out_shape=jax.ShapeDtypeStruct((layers, servers * rows, width), jnp.bfloat16),
        in_specs=[
            pl.BlockSpec(memory_space=pltpu.SMEM),
            pl.BlockSpec(memory_space=pltpu.HBM),
            pl.BlockSpec(memory_space=pltpu.HBM),
        ],
        out_specs=pl.BlockSpec(memory_space=pltpu.HBM),
        scratch_shapes=[
            pltpu.VMEM((layers, ranks, width), jnp.bfloat16),
            pltpu.VMEM((servers, chunk, rows, BLOCK), jnp.bfloat16),
            pltpu.VMEM((layers, servers * rows, width), jnp.bfloat16),
            pltpu.SemaphoreType.DMA((1,)),
            pltpu.SemaphoreType.DMA((servers,)),
            pltpu.SemaphoreType.DMA((1,)),
        ],
        compiler_params=pltpu.CompilerParams(vmem_limit_bytes=VMEM_BYTES),
        name="merge",
    )(order, received, up)


def per_device(base_projection, down_factor_transposed, up_factor, block_permutation):
    servers = lax.axis_size("tp")
    up = lax.all_gather(up_factor, "fsdp", axis=1, tiled=True)
    packed = pack(block_permutation, base_projection, down_factor_transposed.reshape(-1, BLOCK), servers)
    received = lax.cond(
        lax.axis_index("tp") < servers,
        lambda sent: lax.all_to_all(sent, "tp", split_axis=0, concat_axis=0, tiled=True),
        lambda sent: jnp.zeros_like(sent),
        packed,
    )
    return merge(block_permutation, received, up)


def solution(mesh):
    return jax.shard_map(
        per_device,
        mesh=mesh,
        in_specs=(
            P(None, ("fsdp", "tp"), None),
            P(None, None, ("fsdp", "tp")),
            P(None, "fsdp", None),
            P(),
        ),
        out_specs=P(None, "fsdp", "tp"),
        check_vma=False,
    )
```

```python
import jax
import jax.numpy as jnp
from jax import lax
from jax.experimental import pallas as pl
from jax.experimental.pallas import tpu as pltpu
from jax.sharding import PartitionSpec as P

BLOCK = 128
STRIPE = 32
SOURCES = 2
COLUMNS = 3


def block_at(order, j):
    return pl.ds(pl.multiple_of(order[j] * BLOCK, BLOCK), BLOCK)


def pack(order, base, down, servers):
    layers, rows, columns = base.shape
    per_server = order.shape[0] // servers
    chunk = layers * per_server + 1
    stripes = rows // STRIPE

    def kernel(order, base, down, packed, held, load_sem):
        def load(s):
            return pltpu.make_async_copy(
                base.at[s // stripes, pl.ds(s % stripes * STRIPE, STRIPE)], held.at[s], load_sem.at[s]
            )

        for s in range(layers * stripes):
            load(s).start()
        for d in range(servers):
            packed[d, chunk - 1] = down[...]
        for s in range(layers * stripes):
            layer, at = s // stripes, pl.ds(s % stripes * STRIPE, STRIPE)
            load(s).wait()

            @pl.loop(0, servers)
            def _(d):
                for c in range(per_server):
                    packed[d, layer * per_server + c, at] = held[s, :, block_at(order, d * per_server + c)]

    return pl.pallas_call(
        kernel,
        out_shape=pltpu.VMEM((servers, chunk, rows, BLOCK), jnp.bfloat16),
        in_specs=[
            pl.BlockSpec(memory_space=pltpu.SMEM),
            pl.BlockSpec(memory_space=pltpu.HBM),
            pl.BlockSpec(memory_space=pltpu.VMEM),
        ],
        out_specs=pl.BlockSpec(memory_space=pltpu.VMEM),
        scratch_shapes=[
            pltpu.VMEM((layers * stripes, STRIPE, columns), jnp.bfloat16),
            pltpu.SemaphoreType.DMA((layers * stripes,)),
        ],
        compiler_params=pltpu.CompilerParams(vmem_limit_bytes=40 << 20),
        name="pack",
    )(order, base, down)


def merge(order, received, up):
    servers, chunk, rows, _ = received.shape
    layers, ranks, _ = up.shape
    per_server = (chunk - 1) // layers
    width = per_server * BLOCK

    def kernel(order, received, up, out, chosen, held, merged, up_sem, load_sem, store_sem):
        first = lax.axis_index("tp") * per_server
        for c in range(per_server):
            pltpu.make_async_copy(
                up.at[:, :, block_at(order, first + c)],
                chosen.at[:, :, pl.ds(c * BLOCK, BLOCK)],
                up_sem.at[0],
            ).start()

        def load(s):
            return pltpu.make_async_copy(received.at[s], held.at[s], load_sem.at[s])

        for s in range(servers):
            load(s).start()
        pltpu.make_async_copy(chosen, chosen, up_sem.at[0]).wait()

        @pl.loop(0, servers // SOURCES)
        def _(step):
            sources = [step * SOURCES + i for i in range(SOURCES)]
            for s in sources:
                load(s).wait()
            for layer in range(layers):
                down = jnp.concatenate(
                    [held[s, chunk - 1, layer * ranks : (layer + 1) * ranks] for s in sources], axis=1
                ) * jnp.bfloat16(2)
                for c in range(0, per_server, COLUMNS):
                    delta = lax.dot_general(
                        down,
                        chosen[layer, :, c * BLOCK : (c + COLUMNS) * BLOCK],
                        (((0,), (0,)), ((), ())),
                        preferred_element_type=jnp.float32,
                    )
                    for i, s in enumerate(sources):
                        for j in range(COLUMNS):
                            base = held[s, layer * per_server + c + j].astype(jnp.float32)
                            part = delta[i * rows : (i + 1) * rows, j * BLOCK : (j + 1) * BLOCK]
                            at = pl.ds(pl.multiple_of(s * rows, rows), rows)
                            merged[layer, at, (c + j) * BLOCK : (c + j + 1) * BLOCK] = (base + part).astype(jnp.bfloat16)
            at = pl.ds(pl.multiple_of(step * SOURCES * rows, rows), SOURCES * rows)
            pltpu.make_async_copy(merged.at[:, at], out.at[:, at], store_sem.at[0]).start()

        pltpu.make_async_copy(merged, out, store_sem.at[0]).wait()

    return pl.pallas_call(
        kernel,
        out_shape=jax.ShapeDtypeStruct((layers, servers * rows, width), jnp.bfloat16),
        in_specs=[
            pl.BlockSpec(memory_space=pltpu.SMEM),
            pl.BlockSpec(memory_space=pltpu.HBM),
            pl.BlockSpec(memory_space=pltpu.HBM),
        ],
        out_specs=pl.BlockSpec(memory_space=pltpu.HBM),
        scratch_shapes=[
            pltpu.VMEM((layers, ranks, width), jnp.bfloat16),
            pltpu.VMEM((servers, chunk, rows, BLOCK), jnp.bfloat16),
            pltpu.VMEM((layers, servers * rows, width), jnp.bfloat16),
            pltpu.SemaphoreType.DMA((1,)),
            pltpu.SemaphoreType.DMA((servers,)),
            pltpu.SemaphoreType.DMA((1,)),
        ],
        compiler_params=pltpu.CompilerParams(vmem_limit_bytes=60 << 20),
        name="merge",
    )(order, received, up)


def per_device(base_projection, down_factor_transposed, up_factor, block_permutation):
    servers = lax.axis_size("tp")
    up = lax.all_gather(up_factor, "fsdp", axis=1, tiled=True)
    down = down_factor_transposed.reshape(-1, BLOCK)

    def exchange(order, base, down):
        packed = pack(order, base, down, servers)
        return lax.all_to_all(packed, "tp", split_axis=0, concat_axis=0, tiled=True)

    def nothing(order, base, down):
        layers, rows, columns = base.shape
        blocks = layers * columns // BLOCK // servers + 1
        return jnp.zeros((servers, blocks, rows, BLOCK), jnp.bfloat16)

    received = lax.cond(
        lax.axis_index("tp") < servers, exchange, nothing, block_permutation, base_projection, down
    )
    return merge(block_permutation, received, up)


def solution(mesh):
    return jax.shard_map(
        per_device,
        mesh=mesh,
        in_specs=(
            P(None, ("fsdp", "tp"), None),
            P(None, None, ("fsdp", "tp")),
            P(None, "fsdp", None),
            P(),
        ),
        out_specs=P(None, "fsdp", "tp"),
        check_vma=False,
    )
```

```python
import jax
import jax.numpy as jnp
from jax import lax
from jax.experimental import pallas as pl
from jax.experimental.pallas import tpu as pltpu
from jax.sharding import PartitionSpec as P

BLOCK = 128
STRIPE = 32
SOURCES = 4
COLUMNS = 3


def block_at(order, j):
    return pl.ds(pl.multiple_of(order[j] * BLOCK, BLOCK), BLOCK)


def pack(order, base, servers):
    layers, rows, columns = base.shape
    per_server = order.shape[0] // servers
    chunk = layers * per_server
    stripes = rows // STRIPE

    def kernel(order, base, packed, held, load_sem):
        def load(s):
            return pltpu.make_async_copy(
                base.at[s // stripes, pl.ds(s % stripes * STRIPE, STRIPE)], held.at[s], load_sem.at[s]
            )

        for s in range(layers * stripes):
            load(s).start()
        for s in range(layers * stripes):
            layer, at = s // stripes, pl.ds(s % stripes * STRIPE, STRIPE)
            load(s).wait()

            @pl.loop(0, servers, unroll=4)
            def _(d):
                for c in range(per_server):
                    packed[d, layer * per_server + c, at] = held[s, :, block_at(order, d * per_server + c)]

    return pl.pallas_call(
        kernel,
        out_shape=pltpu.VMEM((servers, chunk, rows, BLOCK), jnp.bfloat16),
        in_specs=[
            pl.BlockSpec(memory_space=pltpu.SMEM),
            pl.BlockSpec(memory_space=pltpu.HBM),
        ],
        out_specs=pl.BlockSpec(memory_space=pltpu.VMEM),
        scratch_shapes=[
            pltpu.VMEM((layers * stripes, STRIPE, columns), jnp.bfloat16),
            pltpu.SemaphoreType.DMA((layers * stripes,)),
        ],
        compiler_params=pltpu.CompilerParams(vmem_limit_bytes=40 << 20),
        name="pack",
    )(order, base)


def merge(order, received, up, down):
    servers, chunk, rows, _ = received.shape
    layers, ranks, _ = up.shape
    per_server = chunk // layers
    width = per_server * BLOCK

    def kernel(order, received, up, downs, out, chosen, factor, held, merged, up_sem, down_sem, load_sem, store_sem):
        first = lax.axis_index("tp") * per_server
        for c in range(per_server):
            pltpu.make_async_copy(
                up.at[:, :, block_at(order, first + c)],
                chosen.at[:, :, pl.ds(c * BLOCK, BLOCK)],
                up_sem.at[0],
            ).start()

        rank_rows = pl.ds(lax.axis_index("fsdp") % 2 * servers, servers)
        load_down = pltpu.make_async_copy(downs.at[rank_rows], factor, down_sem.at[0])
        load_down.start()

        def load(s):
            return pltpu.make_async_copy(received.at[s], held.at[s], load_sem.at[s])

        for s in range(servers):
            load(s).start()
        pltpu.make_async_copy(chosen, chosen, up_sem.at[0]).wait()
        load_down.wait()

        @pl.loop(0, servers // SOURCES)
        def _(step):
            sources = [step * SOURCES + i for i in range(SOURCES)]
            for s in sources:
                load(s).wait()
            for layer in range(layers):
                down = jnp.concatenate(
                    [factor[s, layer * ranks : (layer + 1) * ranks] for s in sources], axis=1
                ) * jnp.bfloat16(2)
                for c in range(0, per_server, COLUMNS):
                    delta = lax.dot_general(
                        down,
                        chosen[layer, :, c * BLOCK : (c + COLUMNS) * BLOCK],
                        (((0,), (0,)), ((), ())),
                        preferred_element_type=jnp.float32,
                    )
                    for i, s in enumerate(sources):
                        for j in range(COLUMNS):
                            base = held[s, layer * per_server + c + j].astype(jnp.float32)
                            part = delta[i * rows : (i + 1) * rows, j * BLOCK : (j + 1) * BLOCK]
                            at = pl.ds(pl.multiple_of(s * rows, rows), rows)
                            merged[layer, at, (c + j) * BLOCK : (c + j + 1) * BLOCK] = (base + part).astype(jnp.bfloat16)
                at = pl.ds(pl.multiple_of(step * SOURCES * rows, rows), SOURCES * rows)
                pltpu.make_async_copy(merged.at[layer, at], out.at[layer, at], store_sem.at[0]).start()

        pltpu.make_async_copy(merged, out, store_sem.at[0]).wait()

    return pl.pallas_call(
        kernel,
        out_shape=jax.ShapeDtypeStruct((layers, servers * rows, width), jnp.bfloat16),
        in_specs=[
            pl.BlockSpec(memory_space=pltpu.SMEM),
            pl.BlockSpec(memory_space=pltpu.HBM),
            pl.BlockSpec(memory_space=pltpu.HBM),
            pl.BlockSpec(memory_space=pltpu.HBM),
        ],
        out_specs=pl.BlockSpec(memory_space=pltpu.HBM),
        scratch_shapes=[
            pltpu.VMEM((layers, ranks, width), jnp.bfloat16),
            pltpu.VMEM((servers, layers * ranks, rows), jnp.bfloat16),
            pltpu.VMEM((servers, chunk, rows, BLOCK), jnp.bfloat16),
            pltpu.VMEM((layers, servers * rows, width), jnp.bfloat16),
            pltpu.SemaphoreType.DMA((1,)),
            pltpu.SemaphoreType.DMA((1,)),
            pltpu.SemaphoreType.DMA((servers,)),
            pltpu.SemaphoreType.DMA((1,)),
        ],
        compiler_params=pltpu.CompilerParams(vmem_limit_bytes=60 << 20),
        name="merge",
    )(order, received, up, down)


def per_device(base_projection, down_factor_transposed, up_factor, block_permutation):
    servers = lax.axis_size("tp")
    up = lax.all_gather(up_factor, "fsdp", axis=1, tiled=True)
    layers, ranks, rows = down_factor_transposed.shape
    pairs = lax.axis_size("fsdp") // 2
    group = 2 * servers
    down = lax.all_gather(
        down_factor_transposed.reshape(layers * ranks, rows),
        ("fsdp", "tp"),
        axis=0,
        tiled=True,
        axis_index_groups=[[p * group + i for i in range(group)] for p in range(pairs)],
    ).reshape(group, layers * ranks, rows)

    def exchange(order, base):
        packed = pack(order, base, servers)
        return lax.all_to_all(packed, "tp", split_axis=0, concat_axis=0, tiled=True)

    def nothing(order, base):
        blocks = layers * base.shape[2] // BLOCK // servers
        return jnp.zeros((servers, blocks, rows, BLOCK), jnp.bfloat16)

    received = lax.cond(lax.axis_index("tp") < servers, exchange, nothing, block_permutation, base_projection)
    return merge(block_permutation, received, up, down)


def solution(mesh):
    return jax.shard_map(
        per_device,
        mesh=mesh,
        in_specs=(
            P(None, ("fsdp", "tp"), None),
            P(None, None, ("fsdp", "tp")),
            P(None, "fsdp", None),
            P(),
        ),
        out_specs=P(None, "fsdp", "tp"),
        check_vma=False,
    )
```

```python
import jax
import jax.numpy as jnp
from jax import lax
from jax.experimental import pallas as pl
from jax.experimental.pallas import tpu as pltpu
from jax.sharding import PartitionSpec as P

BLOCK = 128
STRIPE = 32
SOURCES = 4
COLUMNS = 3


def block_at(order, j):
    return pl.ds(pl.multiple_of(order[j] * BLOCK, BLOCK), BLOCK)


def pack(order, base, servers):
    layers, rows, columns = base.shape
    per_server = order.shape[0] // servers
    chunk = layers * per_server
    stripes = rows // STRIPE

    def kernel(order, base, packed, held, load_sem):
        def load(s):
            return pltpu.make_async_copy(
                base.at[s // stripes, pl.ds(s % stripes * STRIPE, STRIPE)], held.at[s], load_sem.at[s]
            )

        for s in range(layers * stripes):
            load(s).start()
        for s in range(layers * stripes):
            layer, at = s // stripes, pl.ds(s % stripes * STRIPE, STRIPE)
            load(s).wait()

            @pl.loop(0, servers, unroll=4)
            def _(d):
                for c in range(per_server):
                    packed[d, layer * per_server + c, at] = held[s, :, block_at(order, d * per_server + c)]

    return pl.pallas_call(
        kernel,
        out_shape=pltpu.VMEM((servers, chunk, rows, BLOCK), jnp.bfloat16),
        in_specs=[
            pl.BlockSpec(memory_space=pltpu.SMEM),
            pl.BlockSpec(memory_space=pltpu.HBM),
        ],
        out_specs=pl.BlockSpec(memory_space=pltpu.VMEM),
        scratch_shapes=[
            pltpu.VMEM((layers * stripes, STRIPE, columns), jnp.bfloat16),
            pltpu.SemaphoreType.DMA((layers * stripes,)),
        ],
        compiler_params=pltpu.CompilerParams(vmem_limit_bytes=40 << 20),
        name="pack",
    )(order, base)


def merge(order, received, up, down):
    servers, chunk, rows, _ = received.shape
    layers, ranks, _ = up.shape
    per_server = chunk // layers
    width = per_server * BLOCK

    def kernel(order, received, up, downs, out, chosen, factor, held, merged, up_sem, down_sem, load_sem, store_sem):
        first = lax.axis_index("tp") * per_server
        for c in range(per_server):
            pltpu.make_async_copy(
                up.at[:, :, block_at(order, first + c)],
                chosen.at[:, :, pl.ds(c * BLOCK, BLOCK)],
                up_sem.at[0],
            ).start()

        core = lax.axis_index("fsdp") % 2
        for s in range(servers):
            pltpu.make_async_copy(downs.at[2 * s + core], factor.at[s], down_sem.at[0]).start()

        def load(s):
            return pltpu.make_async_copy(received.at[s], held.at[s], load_sem.at[s])

        for s in range(servers):
            load(s).start()
        pltpu.make_async_copy(chosen, chosen, up_sem.at[0]).wait()
        pltpu.make_async_copy(factor, factor, down_sem.at[0]).wait()

        @pl.loop(0, servers // SOURCES)
        def _(step):
            sources = [step * SOURCES + i for i in range(SOURCES)]
            for s in sources:
                load(s).wait()
            for layer in range(layers):
                down = jnp.concatenate(
                    [factor[s, layer * ranks : (layer + 1) * ranks] for s in sources], axis=1
                ) * jnp.bfloat16(2)
                for c in range(0, per_server, COLUMNS):
                    delta = lax.dot_general(
                        down,
                        chosen[layer, :, c * BLOCK : (c + COLUMNS) * BLOCK],
                        (((0,), (0,)), ((), ())),
                        preferred_element_type=jnp.float32,
                    )
                    for i, s in enumerate(sources):
                        for j in range(COLUMNS):
                            base = held[s, layer * per_server + c + j].astype(jnp.float32)
                            part = delta[i * rows : (i + 1) * rows, j * BLOCK : (j + 1) * BLOCK]
                            at = pl.ds(pl.multiple_of(s * rows, rows), rows)
                            merged[layer, at, (c + j) * BLOCK : (c + j + 1) * BLOCK] = (base + part).astype(jnp.bfloat16)
                at = pl.ds(pl.multiple_of(step * SOURCES * rows, rows), SOURCES * rows)
                pltpu.make_async_copy(merged.at[layer, at], out.at[layer, at], store_sem.at[0]).start()

        pltpu.make_async_copy(merged, out, store_sem.at[0]).wait()

    return pl.pallas_call(
        kernel,
        out_shape=jax.ShapeDtypeStruct((layers, servers * rows, width), jnp.bfloat16),
        in_specs=[
            pl.BlockSpec(memory_space=pltpu.SMEM),
            pl.BlockSpec(memory_space=pltpu.HBM),
            pl.BlockSpec(memory_space=pltpu.HBM),
            pl.BlockSpec(memory_space=pltpu.HBM),
        ],
        out_specs=pl.BlockSpec(memory_space=pltpu.HBM),
        scratch_shapes=[
            pltpu.VMEM((layers, ranks, width), jnp.bfloat16),
            pltpu.VMEM((servers, layers * ranks, rows), jnp.bfloat16),
            pltpu.VMEM((servers, chunk, rows, BLOCK), jnp.bfloat16),
            pltpu.VMEM((layers, servers * rows, width), jnp.bfloat16),
            pltpu.SemaphoreType.DMA((1,)),
            pltpu.SemaphoreType.DMA((1,)),
            pltpu.SemaphoreType.DMA((servers,)),
            pltpu.SemaphoreType.DMA((1,)),
        ],
        compiler_params=pltpu.CompilerParams(vmem_limit_bytes=60 << 20),
        name="merge",
    )(order, received, up, down)


def per_device(base_projection, down_factor_transposed, up_factor, block_permutation):
    servers = lax.axis_size("tp")
    up = lax.all_gather(up_factor, "fsdp", axis=1, tiled=True)
    layers, ranks, rows = down_factor_transposed.shape
    pairs = lax.axis_size("fsdp") // 2
    group = 2 * servers
    down = lax.all_gather(
        down_factor_transposed.reshape(layers * ranks, rows),
        ("fsdp", "tp"),
        axis=0,
        tiled=True,
        axis_index_groups=[
            [(2 * p + core) * servers + t for t in range(servers) for core in range(2)] for p in range(pairs)
        ],
    ).reshape(group, layers * ranks, rows)

    def exchange(order, base):
        packed = pack(order, base, servers)
        return lax.all_to_all(packed, "tp", split_axis=0, concat_axis=0, tiled=True)

    def nothing(order, base):
        blocks = layers * base.shape[2] // BLOCK // servers
        return jnp.zeros((servers, blocks, rows, BLOCK), jnp.bfloat16)

    received = lax.cond(lax.axis_index("tp") < servers, exchange, nothing, block_permutation, base_projection)
    return merge(block_permutation, received, up, down)


def solution(mesh):
    return jax.shard_map(
        per_device,
        mesh=mesh,
        in_specs=(
            P(None, ("fsdp", "tp"), None),
            P(None, None, ("fsdp", "tp")),
            P(None, "fsdp", None),
            P(),
        ),
        out_specs=P(None, "fsdp", "tp"),
        check_vma=False,
    )
```

```python
import jax
import jax.numpy as jnp
from jax import lax
from jax.experimental import pallas as pl
from jax.experimental.pallas import tpu as pltpu
from jax.sharding import PartitionSpec as P

BLOCK = 128
STRIPE = 32
SOURCES = 4
COLUMNS = 3


def block_at(order, j):
    return pl.ds(pl.multiple_of(order[j] * BLOCK, BLOCK), BLOCK)


def pack(order, base, servers):
    layers, rows, columns = base.shape
    per_server = order.shape[0] // servers
    chunk = layers * per_server
    stripes = rows // STRIPE

    def kernel(order, base, packed, held, load_sem):
        def load(s):
            return pltpu.make_async_copy(
                base.at[s // stripes, pl.ds(s % stripes * STRIPE, STRIPE)], held.at[s], load_sem.at[s]
            )

        for s in range(layers * stripes):
            load(s).start()
        for s in range(layers * stripes):
            layer, at = s // stripes, pl.ds(s % stripes * STRIPE, STRIPE)
            load(s).wait()

            @pl.loop(0, servers, unroll=4)
            def _(d):
                for c in range(per_server):
                    packed[d, layer * per_server + c, at] = held[s, :, block_at(order, d * per_server + c)]

    return pl.pallas_call(
        kernel,
        out_shape=pltpu.VMEM((servers, chunk, rows, BLOCK), jnp.bfloat16),
        in_specs=[
            pl.BlockSpec(memory_space=pltpu.SMEM),
            pl.BlockSpec(memory_space=pltpu.HBM),
        ],
        out_specs=pl.BlockSpec(memory_space=pltpu.VMEM),
        scratch_shapes=[
            pltpu.VMEM((layers * stripes, STRIPE, columns), jnp.bfloat16),
            pltpu.SemaphoreType.DMA((layers * stripes,)),
        ],
        compiler_params=pltpu.CompilerParams(vmem_limit_bytes=40 << 20),
        name="pack",
    )(order, base)


def merge(order, received, up, down):
    servers, chunk, rows, _ = received.shape
    layers, ranks, _ = up.shape
    per_server = chunk // layers
    width = per_server * BLOCK

    def kernel(order, received, up, downs, out, chosen, factor, held, merged, up_sem, down_sem, load_sem, store_sem):
        first = lax.axis_index("tp") * per_server
        for c in range(per_server):
            pltpu.make_async_copy(
                up.at[:, :, block_at(order, first + c)],
                chosen.at[:, :, pl.ds(c * BLOCK, BLOCK)],
                up_sem.at[0],
            ).start()

        core = lax.axis_index("fsdp") % 2
        for s in range(servers):
            pltpu.make_async_copy(downs.at[2 * s + core], factor.at[s], down_sem.at[0]).start()

        def load(s):
            return pltpu.make_async_copy(received.at[s], held.at[s], load_sem.at[s])

        for s in range(servers):
            load(s).start()
        pltpu.make_async_copy(chosen, chosen, up_sem.at[0]).wait()
        pltpu.make_async_copy(factor, factor, down_sem.at[0]).wait()

        @pl.loop(0, servers // SOURCES)
        def _(step):
            sources = [step * SOURCES + i for i in range(SOURCES)]
            for s in sources:
                load(s).wait()
            for layer in range(layers):
                down = jnp.concatenate(
                    [factor[s, layer * ranks : (layer + 1) * ranks] for s in sources], axis=1
                ) * jnp.bfloat16(2)
                for c in range(0, per_server, COLUMNS):
                    delta = lax.dot_general(
                        down,
                        chosen[layer, :, c * BLOCK : (c + COLUMNS) * BLOCK],
                        (((0,), (0,)), ((), ())),
                        preferred_element_type=jnp.float32,
                    )
                    for i, s in enumerate(sources):
                        for j in range(COLUMNS):
                            base = held[s, layer * per_server + c + j].astype(jnp.float32)
                            part = delta[i * rows : (i + 1) * rows, j * BLOCK : (j + 1) * BLOCK]
                            at = pl.ds(pl.multiple_of(s * rows, rows), rows)
                            merged[layer, at, (c + j) * BLOCK : (c + j + 1) * BLOCK] = (base + part).astype(jnp.bfloat16)
                    at = pl.ds(pl.multiple_of(step * SOURCES * rows, rows), SOURCES * rows)
                    cols = pl.ds(c * BLOCK, COLUMNS * BLOCK)
                    pltpu.make_async_copy(merged.at[layer, at, cols], out.at[layer, at, cols], store_sem.at[0]).start()

        pltpu.make_async_copy(merged, out, store_sem.at[0]).wait()

    return pl.pallas_call(
        kernel,
        out_shape=jax.ShapeDtypeStruct((layers, servers * rows, width), jnp.bfloat16),
        in_specs=[
            pl.BlockSpec(memory_space=pltpu.SMEM),
            pl.BlockSpec(memory_space=pltpu.HBM),
            pl.BlockSpec(memory_space=pltpu.HBM),
            pl.BlockSpec(memory_space=pltpu.HBM),
        ],
        out_specs=pl.BlockSpec(memory_space=pltpu.HBM),
        scratch_shapes=[
            pltpu.VMEM((layers, ranks, width), jnp.bfloat16),
            pltpu.VMEM((servers, layers * ranks, rows), jnp.bfloat16),
            pltpu.VMEM((servers, chunk, rows, BLOCK), jnp.bfloat16),
            pltpu.VMEM((layers, servers * rows, width), jnp.bfloat16),
            pltpu.SemaphoreType.DMA((1,)),
            pltpu.SemaphoreType.DMA((1,)),
            pltpu.SemaphoreType.DMA((servers,)),
            pltpu.SemaphoreType.DMA((1,)),
        ],
        compiler_params=pltpu.CompilerParams(vmem_limit_bytes=60 << 20),
        name="merge",
    )(order, received, up, down)


def per_device(base_projection, down_factor_transposed, up_factor, block_permutation):
    servers = lax.axis_size("tp")
    up = lax.all_gather(up_factor, "fsdp", axis=1, tiled=True)
    layers, ranks, rows = down_factor_transposed.shape
    pairs = lax.axis_size("fsdp") // 2
    group = 2 * servers
    down = lax.all_gather(
        down_factor_transposed.reshape(layers * ranks, rows),
        ("fsdp", "tp"),
        axis=0,
        tiled=True,
        axis_index_groups=[
            [(2 * p + core) * servers + t for t in range(servers) for core in range(2)] for p in range(pairs)
        ],
    ).reshape(group, layers * ranks, rows)

    def exchange(order, base):
        packed = pack(order, base, servers)
        return lax.all_to_all(packed, "tp", split_axis=0, concat_axis=0, tiled=True)

    def nothing(order, base):
        blocks = layers * base.shape[2] // BLOCK // servers
        return jnp.zeros((servers, blocks, rows, BLOCK), jnp.bfloat16)

    received = lax.cond(lax.axis_index("tp") < servers, exchange, nothing, block_permutation, base_projection)
    return merge(block_permutation, received, up, down)


def solution(mesh):
    return jax.shard_map(
        per_device,
        mesh=mesh,
        in_specs=(
            P(None, ("fsdp", "tp"), None),
            P(None, None, ("fsdp", "tp")),
            P(None, "fsdp", None),
            P(),
        ),
        out_specs=P(None, "fsdp", "tp"),
        check_vma=False,
    )
```

```python
import jax
import jax.numpy as jnp
from jax import lax
from jax.experimental import pallas as pl
from jax.experimental.pallas import tpu as pltpu
from jax.sharding import PartitionSpec as P

BLOCK = 128
STRIPE = 32
SOURCES = 4
COLUMNS = 3


def block_at(order, j):
    return pl.ds(pl.multiple_of(order[j] * BLOCK, BLOCK), BLOCK)


def pack(order, base, servers):
    layers, rows, columns = base.shape
    per_server = order.shape[0] // servers
    chunk = layers * per_server
    stripes = rows // STRIPE

    pieces = [(s // stripes, s % stripes * STRIPE, STRIPE) for s in range(layers * stripes)]
    layer, row, size = pieces.pop()
    pieces += [(layer, row, size // 2), (layer, row + size // 2, size // 2)]

    def kernel(order, base, packed, held, load_sem):
        def load(s):
            layer, row, size = pieces[s]
            at = pl.ds(row, size)
            return pltpu.make_async_copy(base.at[layer, at], held.at[layer, at], load_sem.at[s])

        for s in range(len(pieces)):
            load(s).start()
        for s, (layer, row, size) in enumerate(pieces):
            at = pl.ds(row, size)
            load(s).wait()

            @pl.loop(0, servers, unroll=4)
            def _(d):
                for c in range(per_server):
                    packed[d, layer * per_server + c, at] = held[layer, at, block_at(order, d * per_server + c)]

    return pl.pallas_call(
        kernel,
        out_shape=pltpu.VMEM((servers, chunk, rows, BLOCK), jnp.bfloat16),
        in_specs=[
            pl.BlockSpec(memory_space=pltpu.SMEM),
            pl.BlockSpec(memory_space=pltpu.HBM),
        ],
        out_specs=pl.BlockSpec(memory_space=pltpu.VMEM),
        scratch_shapes=[
            pltpu.VMEM((layers, rows, columns), jnp.bfloat16),
            pltpu.SemaphoreType.DMA((len(pieces),)),
        ],
        compiler_params=pltpu.CompilerParams(vmem_limit_bytes=40 << 20),
        name="pack",
    )(order, base)


def merge(order, received, up, down):
    servers, chunk, rows, _ = received.shape
    layers, ranks, _ = up.shape
    per_server = chunk // layers
    width = per_server * BLOCK

    def kernel(order, received, up, downs, out, chosen, factor, held, merged, up_sem, down_sem, load_sem, store_sem):
        first = lax.axis_index("tp") * per_server
        for c in range(per_server):
            pltpu.make_async_copy(
                up.at[:, :, block_at(order, first + c)],
                chosen.at[:, :, pl.ds(c * BLOCK, BLOCK)],
                up_sem.at[0],
            ).start()

        core = lax.axis_index("fsdp") % 2
        for s in range(servers):
            pltpu.make_async_copy(downs.at[2 * s + core], factor.at[s], down_sem.at[0]).start()

        def load(s):
            return pltpu.make_async_copy(received.at[s], held.at[s], load_sem.at[s])

        for s in range(servers):
            load(s).start()
        pltpu.make_async_copy(chosen, chosen, up_sem.at[0]).wait()
        pltpu.make_async_copy(factor, factor, down_sem.at[0]).wait()

        @pl.loop(0, servers // SOURCES)
        def _(step):
            sources = [step * SOURCES + i for i in range(SOURCES)]
            for s in sources:
                load(s).wait()
            for layer in range(layers):
                down = jnp.concatenate(
                    [factor[s, layer * ranks : (layer + 1) * ranks] for s in sources], axis=1
                ) * jnp.bfloat16(2)
                for c in range(0, per_server, COLUMNS):
                    delta = lax.dot_general(
                        down,
                        chosen[layer, :, c * BLOCK : (c + COLUMNS) * BLOCK],
                        (((0,), (0,)), ((), ())),
                        preferred_element_type=jnp.float32,
                    )
                    for i, s in enumerate(sources):
                        for j in range(COLUMNS):
                            base = held[s, layer * per_server + c + j].astype(jnp.float32)
                            part = delta[i * rows : (i + 1) * rows, j * BLOCK : (j + 1) * BLOCK]
                            at = pl.ds(pl.multiple_of(s * rows, rows), rows)
                            merged[layer, at, (c + j) * BLOCK : (c + j + 1) * BLOCK] = (base + part).astype(jnp.bfloat16)
                    at = pl.ds(pl.multiple_of(step * SOURCES * rows, rows), SOURCES * rows)
                    cols = pl.ds(c * BLOCK, COLUMNS * BLOCK)
                    pltpu.make_async_copy(merged.at[layer, at, cols], out.at[layer, at, cols], store_sem.at[0]).start()

        pltpu.make_async_copy(merged, out, store_sem.at[0]).wait()

    return pl.pallas_call(
        kernel,
        out_shape=jax.ShapeDtypeStruct((layers, servers * rows, width), jnp.bfloat16),
        in_specs=[
            pl.BlockSpec(memory_space=pltpu.SMEM),
            pl.BlockSpec(memory_space=pltpu.HBM),
            pl.BlockSpec(memory_space=pltpu.HBM),
            pl.BlockSpec(memory_space=pltpu.HBM),
        ],
        out_specs=pl.BlockSpec(memory_space=pltpu.HBM),
        scratch_shapes=[
            pltpu.VMEM((layers, ranks, width), jnp.bfloat16),
            pltpu.VMEM((servers, layers * ranks, rows), jnp.bfloat16),
            pltpu.VMEM((servers, chunk, rows, BLOCK), jnp.bfloat16),
            pltpu.VMEM((layers, servers * rows, width), jnp.bfloat16),
            pltpu.SemaphoreType.DMA((1,)),
            pltpu.SemaphoreType.DMA((1,)),
            pltpu.SemaphoreType.DMA((servers,)),
            pltpu.SemaphoreType.DMA((1,)),
        ],
        compiler_params=pltpu.CompilerParams(vmem_limit_bytes=60 << 20),
        name="merge",
    )(order, received, up, down)


def per_device(base_projection, down_factor_transposed, up_factor, block_permutation):
    servers = lax.axis_size("tp")
    up = lax.all_gather(up_factor, "fsdp", axis=1, tiled=True)
    layers, ranks, rows = down_factor_transposed.shape
    pairs = lax.axis_size("fsdp") // 2
    group = 2 * servers
    down = lax.all_gather(
        down_factor_transposed.reshape(layers * ranks, rows),
        ("fsdp", "tp"),
        axis=0,
        tiled=True,
        axis_index_groups=[
            [(2 * p + core) * servers + t for t in range(servers) for core in range(2)] for p in range(pairs)
        ],
    ).reshape(group, layers * ranks, rows)

    def exchange(order, base):
        packed = pack(order, base, servers)
        return lax.all_to_all(packed, "tp", split_axis=0, concat_axis=0, tiled=True)

    def nothing(order, base):
        blocks = layers * base.shape[2] // BLOCK // servers
        return jnp.zeros((servers, blocks, rows, BLOCK), jnp.bfloat16)

    received = lax.cond(lax.axis_index("tp") < servers, exchange, nothing, block_permutation, base_projection)
    return merge(block_permutation, received, up, down)


def solution(mesh):
    return jax.shard_map(
        per_device,
        mesh=mesh,
        in_specs=(
            P(None, ("fsdp", "tp"), None),
            P(None, None, ("fsdp", "tp")),
            P(None, "fsdp", None),
            P(),
        ),
        out_specs=P(None, "fsdp", "tp"),
        check_vma=False,
    )
```
